512 devices in a mesh: group: 4 (over y), ep: 128 (over x, z, core).
Axes of the slice: x: 4, y: 4, z: 16, core: 2. Of those that a mesh axis runs over, the one named last changes fastest.
Arguments:
- tokens: bfloat16 [4096, 3584], P('ep'), may hold values from -6 to 6
- expert_ids: int32 [4096, 8], P('ep'), may hold values from 0 to 63, all different within a row; in each aligned block of 8 rows (0 to 7, 8 to 15, ...) at most 2 rows name the same one
- route_weight: float32 [4096, 8], P('ep'), may hold values from 0.05 to 0.5
- w_gate: bfloat16 [128, 3584, 512], P('ep', None, 'group'), may hold values from -0.09375 to 0.09375
- w_up: bfloat16 [128, 3584, 512], P('ep', None, 'group'), may hold values from -0.09375 to 0.09375
- w_down: bfloat16 [128, 512, 3584], P('ep', 'group'), may hold values from -0.1875 to 0.1875
Outputs:
- moe_out: bfloat16 [4096, 3584], P('ep')
The draws below stay inside these ranges and needn't reach their ends.
Inputs may be any that keep to these rules, and one draw needn't show every extreme that they name: `expert_ids`: in each aligned block of 8 rows no expert is named by more than 2 rows, a bound that some block reaches.
All inputs are finite; a program needn't handle non-finite values.
Results may differ from the reference program's by a relative error of at most 0.0057.
Values may be sent and summed in bfloat16 or wider, within the bound.
No kernel may reach another device: no remote copies, remote signals or barrier semaphores. Data moves between devices by JAX's collectives and lax.ppermute only.
A program may use at most 64 MiB of HBM per device.

```python
import math
import jax
import jax.numpy as jnp
import numpy as np
from jax import lax

D = 3584
EXPERT_HIDDEN = 1024
EXPERTS = 64
TOPK = 8
TOKENS = 4096
HALF_HIDDEN = 512
HID_DEV = 128
BLOCK = 8
CAP = 2
SLOT = 8
N_GROUP = 4
N_EP = 128


def level_of(rng, extent, pieces, least, high):
    def one(dim, blocks):
        heights = jax.random.uniform(jax.random.fold_in(jax.random.fold_in(rng, 6), dim), (blocks,), jnp.float32, least / len(pieces), high / len(pieces))
        return jnp.repeat(jnp.exp(heights), extent[dim] // blocks).reshape((-1,) + (1,) * (len(extent) - dim - 1))

    level = one(*pieces[0])
    for cut in pieces[1:]:
        level = level * one(*cut)
    return level


def assign_block(rng, own, number, rows, number_of, top, limit, skew):
    sequence = jax.random.permutation(rng, number_of)
    packed, usual = load_shares(number_of, rows * top, limit, skew, True), load_shares(number_of, rows * top, limit, skew, False)
    places = jnp.arange(number_of)

    def named(tallies, rotation):
        used = int((tallies > 0).sum())
        fixed = max(1, used // 4)
        passed = fixed + (places - fixed + rotation * (used - fixed)) % max(1, number_of - fixed)
        return jnp.zeros((number_of,), jnp.int32).at[sequence[jnp.where(places < fixed, places, passed)]].set(jnp.asarray(tallies, jnp.int32))

    tallies = jnp.where(number % 4 == 0, named(packed, number // 4), named(usual, number - number // 4 - 1))
    mixed = jax.random.permutation(jax.random.fold_in(own, 3), number_of)
    giver, taker = mixed[0:number_of // 2 * 2:2], mixed[1:number_of // 2 * 2:2]
    slack = jnp.minimum(tallies[giver] - 1, limit - tallies[taker]) // 2
    slack = jnp.where((giver == sequence[0]) | (taker == sequence[0]) | (tallies[taker] == 0), 0, jnp.maximum(slack, 0))
    passed = jax.random.randint(jax.random.fold_in(own, 4), (number_of // 2,), 0, 1 << 20) % (slack + 1)
    tallies = tallies.at[giver].add(-passed).at[taker].add(passed)
    items = jnp.searchsorted(jnp.cumsum(tallies), jnp.arange(rows * top), side="right").astype(jnp.int32)
    listing = items.reshape(top, rows).T
    listing = listing[jax.random.permutation(jax.random.fold_in(own, 1), rows)]
    rotation = jax.random.randint(jax.random.fold_in(own, 2), (rows, 1), 0, top)
    return jnp.take_along_axis(listing, (jnp.arange(top)[None, :] + rotation) % top, axis=1)


def load_shares(count, total, bound, lean, full):
    weights = [(1 << 20) // math.isqrt(standing ** lean) + 1 for standing in range(1, count + 1)]
    largest = bound if full else min(bound, max(-(-total // count), total * weights[0] // sum(weights)))
    least = 1 if total - largest >= count - 1 else 0
    counts, rest = [largest] + [least] * (count - 1), total - largest - least * (count - 1)
    while rest > 0:
        movable = [i for i in range(1, count) if counts[i] < largest] or [i for i in range(1, count) if counts[i] < bound]
        whole, left = sum([weights[i] for i in movable]), rest
        for i in movable:
            extra = min(bound - counts[i], max(1, left * weights[i] // whole), rest)
            counts[i] = counts[i] + extra
            rest = rest - extra
    return np.array(counts)


def bell_draw(own_key, extent, scale, bound, shards=(), kind=jnp.bfloat16):
    level = level_of(own_key, extent, shards, -0.22, 0.18) if shards else 1.0
    result = jax.random.normal(own_key, extent, jnp.float32) * scale * level
    return jnp.minimum(jnp.maximum(result, -bound), bound).astype(kind)


def setup_inputs(seed: int = 0) -> dict:
    splits = jax.random.split(jax.random.key(seed), 7)
    tokens = bell_draw(splits[0], (TOKENS, D), 1.0, 6.0, ((0, 128),))
    expert_ids_keys = jax.random.split(jax.random.fold_in(splits[1], 1), TOKENS // BLOCK)
    expert_ids_turns = jax.random.permutation(jax.random.fold_in(splits[1], 3), TOKENS // BLOCK)
    expert_ids = jax.vmap(lambda own, number: assign_block(jax.random.fold_in(splits[1], 2), own, number, BLOCK, EXPERTS, TOPK, CAP, 2))(expert_ids_keys, expert_ids_turns).reshape((TOKENS, TOPK))
    route_weight = jnp.clip(jnp.exp(math.log(0.5) - 2.3025851 * jax.random.uniform(splits[2], (TOKENS, TOPK), jnp.float32) ** level_of(splits[2], (TOKENS, TOPK), ((0, 128),), -0.2, 0.2)), 0.05, 0.5)
    w_gate = bell_draw(splits[3], (2 * EXPERTS, D, HALF_HIDDEN), D ** -0.5, 0.09375, ((0, 128), (2, 4)))
    w_up = bell_draw(splits[4], (2 * EXPERTS, D, HALF_HIDDEN), D ** -0.5, 0.09375, ((0, 128), (2, 4)))
    w_down = bell_draw(splits[5], (2 * EXPERTS, HALF_HIDDEN, D), EXPERT_HIDDEN ** -0.5, 0.1875, ((0, 128), (1, 4)))
    return dict(tokens=tokens, expert_ids=expert_ids, route_weight=route_weight, w_gate=w_gate, w_up=w_up, w_down=w_down)


def reference(tokens, expert_ids, route_weight, w_gate, w_up, w_down):
    part_count = 2 * N_GROUP
    row_limit = N_EP * SLOT
    features = tokens.shape[1]
    padded = jnp.concatenate([tokens, jnp.zeros((1, features), tokens.dtype)], 0)

    def expert_step(totals, expert):
        hit_mask = expert_ids == expert
        chosen = jnp.any(hit_mask, axis=1)
        row_index = jnp.nonzero(chosen, size=row_limit, fill_value=TOKENS)[0].astype(jnp.int32)
        weight = jnp.sum(jnp.where(hit_mask, route_weight, jnp.float32(0.0)), axis=1)
        weight = jnp.concatenate([weight, jnp.zeros((1,), jnp.float32)])[row_index]
        start = (2 * expert).astype(jnp.int32)
        gate_mat = jnp.transpose(lax.dynamic_slice_in_dim(w_gate, start, 2, 0), (1, 0, 2)).reshape(features, EXPERT_HIDDEN)
        up_mat = jnp.transpose(lax.dynamic_slice_in_dim(w_up, start, 2, 0), (1, 0, 2)).reshape(features, EXPERT_HIDDEN)
        down_mat = lax.dynamic_slice_in_dim(w_down, start, 2, 0).reshape(part_count, HID_DEV, features)
        inputs = padded[row_index]
        gate_value = jnp.dot(inputs, gate_mat, preferred_element_type=jnp.float32)
        up_value = jnp.dot(inputs, up_mat, preferred_element_type=jnp.float32)
        act = (jax.nn.silu(gate_value) * up_value).astype(jnp.bfloat16)
        piece = jnp.einsum("rph,phd->rpd", act.reshape(row_limit, part_count, HID_DEV).astype(jnp.float32), down_mat.astype(jnp.float32)).astype(jnp.bfloat16)
        piece = lax.optimization_barrier(piece)
        summed = jnp.sum(piece.astype(jnp.float32), axis=1)
        return totals.at[row_index].add(weight[:, None] * summed), None

    totals, _ = lax.scan(expert_step, jnp.zeros((TOKENS + 1, features), jnp.float32), jnp.arange(EXPERTS, dtype=jnp.int32))
    return totals[:TOKENS].astype(jnp.bfloat16)
```

```python
import jax
import jax.numpy as jnp
from jax import lax
from jax.experimental import pallas as pl
from jax.experimental.pallas import tpu as pltpu
from jax.sharding import Mesh, PartitionSpec as P

BLOCK = 8
CAP = 2
SLOT = 8
MIB = 1 << 20


def params():
    return pltpu.CompilerParams(vmem_limit_bytes=24 * MIB)


def slot_mask(ids, experts):
    tokens, top = ids.shape
    lane = lax.broadcasted_iota(jnp.int32, (tokens, experts), 1)
    hit = jnp.zeros((tokens, experts), jnp.float32)
    for j in range(top):
        hit = hit + jnp.where(ids[:, j:j + 1] == lane, 1.0, 0.0)
    row = lax.broadcasted_iota(jnp.int32, (tokens, tokens), 0)
    col = lax.broadcasted_iota(jnp.int32, (tokens, tokens), 1)
    earlier = jnp.where((row // BLOCK == col // BLOCK) & (col < row), 1.0, 0.0).astype(jnp.bfloat16)
    rank = jnp.dot(earlier, hit.astype(jnp.bfloat16), preferred_element_type=jnp.float32)
    place = lax.broadcasted_iota(jnp.int32, (tokens, experts), 0) // BLOCK * CAP
    code = jnp.where(hit > 0.5, place.astype(jnp.float32) + rank + 1.0, 0.0)
    spread = expand(experts)
    wide = jnp.dot(code.astype(jnp.bfloat16), spread, preferred_element_type=jnp.float32)
    slot = lax.broadcasted_iota(jnp.int32, (tokens, experts * SLOT), 1) % SLOT
    return wide == (slot + 1).astype(jnp.float32)


def expand(experts):
    row = lax.broadcasted_iota(jnp.int32, (experts, experts * SLOT), 0)
    col = lax.broadcasted_iota(jnp.int32, (experts, experts * SLOT), 1)
    return jnp.where(col // SLOT == row, 1.0, 0.0).astype(jnp.bfloat16)


def dispatch_kernel(y_ref, ids_ref, tokens_ref, out_ref):
    experts = out_ref.shape[0] // SLOT
    onehot = jnp.where(slot_mask(ids_ref[...], experts), 1.0, 0.0).astype(jnp.bfloat16)
    rows = lax.dot_general(
        onehot, tokens_ref[...], (((0,), (0,)), ((), ())), preferred_element_type=jnp.float32
    )
    out_ref[...] = rows.astype(jnp.bfloat16)


def dispatch(y, ids, tokens, experts, width):
    count = tokens.shape[0]
    return pl.pallas_call(
        dispatch_kernel,
        grid_spec=pltpu.PrefetchScalarGridSpec(
            num_scalar_prefetch=1,
            grid=(1,),
            in_specs=[
                pl.BlockSpec(ids.shape, lambda i, y: (0, 0)),
                pl.BlockSpec((count, width), lambda i, y: (0, y[0])),
            ],
            out_specs=pl.BlockSpec((experts * SLOT, width), lambda i, y: (0, 0)),
        ),
        out_shape=jax.ShapeDtypeStruct((experts * SLOT, width), tokens.dtype),
        compiler_params=params(),
        name="dispatch_rows",
    )(y, ids, tokens)


def combine_kernel(y_ref, ids_ref, weight_ref, rows_ref, out_ref):
    experts = rows_ref.shape[0] // SLOT
    copies, count, features = out_ref.shape
    width = rows_ref.shape[1]
    quarters = features // width
    ids = jnp.concatenate([ids_ref[...]] * quarters, axis=0)
    weight = jnp.concatenate([weight_ref[...]] * quarters, axis=0)
    tokens, top = ids.shape
    mask = slot_mask(ids, experts)
    lane = lax.broadcasted_iota(jnp.int32, (tokens, experts), 1)
    rest = jnp.zeros((tokens, experts), jnp.float32)
    for j in range(top):
        rest = rest + jnp.where(ids[:, j:j + 1] == lane, weight[:, j:j + 1], 0.0)
    spread = expand(experts)
    total = None
    for _ in range(3):
        part = rest.astype(jnp.bfloat16)
        rest = rest - part.astype(jnp.float32)
        wide = jnp.dot(part, spread, preferred_element_type=jnp.float32)
        wide = jnp.where(mask, wide, 0.0).astype(jnp.bfloat16)
        term = jnp.dot(wide, rows_ref[...], preferred_element_type=jnp.float32)
        total = term if total is None else total + term
    line = jnp.concatenate([total[i * count:(i + 1) * count] for i in range(quarters)], axis=1)
    line = line.astype(jnp.bfloat16)
    for i in range(copies):
        out_ref[i] = line


def combine(y, ids, weight, rows, blocks):
    count, width = ids.shape[0] // blocks, rows.shape[1]
    shape = (blocks, count, blocks * width)
    return pl.pallas_call(
        combine_kernel,
        grid_spec=pltpu.PrefetchScalarGridSpec(
            num_scalar_prefetch=1,
            grid=(1,),
            in_specs=[
                pl.BlockSpec((count, ids.shape[1]), lambda i, y: (y[0], 0)),
                pl.BlockSpec((count, ids.shape[1]), lambda i, y: (y[0], 0)),
                pl.BlockSpec(rows.shape, lambda i, y: (0, 0)),
            ],
            out_specs=pl.BlockSpec(shape, lambda i, y: (0, 0, 0)),
        ),
        out_shape=jax.ShapeDtypeStruct(shape, jnp.bfloat16),
        compiler_params=params(),
        name="combine_rows",
    )(y, ids, weight, rows)


def regroup(rows, blocks, inverse):
    line = lax.broadcasted_iota(jnp.int32, (rows, 1), 0)
    span = rows // blocks
    if inverse:
        index = (line % SLOT) // CAP * span + line // SLOT * CAP + line % CAP
    else:
        index = (line % span) // CAP * SLOT + line // span * CAP + line % CAP
    hit = lax.broadcasted_iota(jnp.int32, (rows, rows), 1) == index
    return jnp.where(hit, 1.0, 0.0).astype(jnp.bfloat16)


def gate_up_kernel(q_ref, x_ref, w0_ref, w1_ref, out_ref, held):
    @pl.when(pl.program_id(0) == 0)
    def _():
        order = regroup(x_ref.shape[0], pl.num_programs(0), False)
        moved = jnp.dot(order, x_ref[...], preferred_element_type=jnp.float32)
        held[...] = moved.astype(jnp.bfloat16)

    hidden = w0_ref.shape[3]
    x = held[...]
    for c, ref in enumerate((w0_ref, w1_ref)):
        w = jnp.concatenate([ref[0, 0], ref[0, 1]], axis=1)
        part = jnp.dot(x, w, preferred_element_type=jnp.float32)
        out_ref[:, 2 * c * hidden:2 * (c + 1) * hidden] = part.astype(jnp.bfloat16)


def gate_up(q, rows, w_own, w_other):
    slots, width = rows.shape
    blocks, _, _, hidden = w_own.shape
    wide = pl.BlockSpec((1, 2, width, hidden), lambda i, q: (i, 0, 0, 0))
    return pl.pallas_call(
        gate_up_kernel,
        grid_spec=pltpu.PrefetchScalarGridSpec(
            num_scalar_prefetch=1,
            grid=(blocks,),
            in_specs=[pl.BlockSpec((slots, width), lambda i, q: (0, 0)), wide, wide],
            out_specs=pl.BlockSpec((slots, 4 * hidden), lambda i, q: (0, q[i])),
            scratch_shapes=[pltpu.VMEM((slots, width), jnp.bfloat16)],
        ),
        out_shape=jax.ShapeDtypeStruct((slots, 4 * blocks * hidden), jnp.bfloat16),
        compiler_params=params(),
        name="gate_up",
    )(q, rows, w_own, w_other)


def down_kernel(q_ref, x_ref, w0_ref, w1_ref, out_ref, act0, act1, held):
    step = pl.program_id(0)
    parts, span, columns = x_ref.shape
    group = columns // parts
    hidden = group // 4

    @pl.when(step == 0)
    def _():
        for i in range(parts):
            start = pl.multiple_of(q_ref[i] * group, group)
            total = None
            for p in range(parts):
                term = x_ref[p, :, pl.ds(start, group)].astype(jnp.float32)
                total = term if total is None else total + term
            for c, act in enumerate((act0, act1)):
                gate = total[:, 2 * c * hidden:(2 * c + 1) * hidden]
                up = total[:, (2 * c + 1) * hidden:(2 * c + 2) * hidden]
                value = gate / (1.0 + jnp.exp(-gate)) * up
                act[:, i * hidden:(i + 1) * hidden] = value.astype(jnp.bfloat16)

    total = jnp.dot(act0[...], w0_ref[...], preferred_element_type=jnp.float32)
    total = total + jnp.dot(act1[...], w1_ref[...], preferred_element_type=jnp.float32)
    held[pl.ds(pl.multiple_of(step * span, span), span)] = total.astype(jnp.bfloat16)

    @pl.when(step == parts - 1)
    def _():
        order = regroup(parts * span, parts, True)
        moved = jnp.dot(order, held[...], preferred_element_type=jnp.float32)
        out_ref[...] = moved.astype(jnp.bfloat16)


def down(q, sums, w_own, w_other):
    parts, span, _ = sums.shape
    depth, features = w_own.shape
    width = features // parts
    part = pl.BlockSpec((depth, width), lambda i, q: (0, i))
    return pl.pallas_call(
        down_kernel,
        grid_spec=pltpu.PrefetchScalarGridSpec(
            num_scalar_prefetch=1,
            grid=(parts,),
            in_specs=[pl.BlockSpec(sums.shape, lambda i, q: (0, 0, 0)), part, part],
            out_specs=pl.BlockSpec((parts * span, width), lambda i, q: (0, 0)),
            scratch_shapes=[
                pltpu.VMEM((span, depth), jnp.bfloat16),
                pltpu.VMEM((span, depth), jnp.bfloat16),
                pltpu.VMEM((parts * span, width), jnp.bfloat16),
            ],
        ),
        out_shape=jax.ShapeDtypeStruct((parts * span, width), jnp.bfloat16),
        compiler_params=params(),
        name="down_rows",
    )(q, sums, w_own, w_other)


def shift(block, step):
    n = lax.axis_size("y")
    return lax.ppermute(block, "y", [(i, (i + step) % n) for i in range(n)])


def swap(block):
    return lax.ppermute(block, "c", [(0, 1), (1, 0)])


def swap_all(block, axis):
    return lax.all_to_all(block, axis, split_axis=0, concat_axis=0, tiled=True)


def per_device(tokens, expert_ids, route_weight, w_gate, w_up, w_down):
    ny = lax.axis_size("y")
    experts = lax.axis_size("x") * lax.axis_size("z")
    y = lax.axis_index("y").astype(jnp.int32)
    q = jnp.stack([y, (y + 3) & 3, (y + 1) & 3, (y + 2) & 3])
    width = tokens.shape[1] // ny
    half = w_down.shape[1] // 2

    sent = dispatch(q[:1], expert_ids, tokens, experts, width)
    sent, w_gate, w_up, w_down = lax.optimization_barrier((sent, w_gate, w_up, w_down))
    rows = swap_all(sent, ("x", "z"))

    def quarter(w, i):
        return lax.dynamic_slice_in_dim(w[0], q[i] * width, width, 0)

    from_before = shift(jnp.stack([quarter(w_gate, 2), quarter(w_up, 2), quarter(w_gate, 3)]), 1)
    from_after = shift(jnp.stack([quarter(w_gate, 1), quarter(w_up, 1), quarter(w_up, 3)]), -1)
    from_before, from_after, w_down = lax.optimization_barrier((from_before, from_after, w_down))
    gate_across, up_across = shift(from_before[2], 1), shift(from_after[2], -1)
    before, after = shift(w_down[0], 1), shift(w_down[0], -1)
    both_own = jnp.stack([
        quarter(w_gate, 0), quarter(w_up, 0), from_before[0], from_before[1],
        from_after[0], from_after[1], gate_across, up_across,
    ]).reshape(ny, 2, width, w_gate.shape[2])
    both_other = swap(both_own)
    across = (shift(before[:half], 1), shift(after[half:], -1))

    sums = gate_up(q, rows, both_own, both_other)
    sums, before, after, across = lax.optimization_barrier((sums, before, after, across))
    w_own = jnp.concatenate([w_down[0], before, after, *across], axis=0)
    w_other = swap(w_own)
    sums = swap_all(sums.reshape(ny, sums.shape[0] // ny, sums.shape[1]), "y")
    back = swap_all(down(q, sums, w_own, w_other), ("x", "z"))
    mine = swap_all(combine(q[:1], expert_ids, route_weight, back, ny), "y")
    return mine.reshape(tokens.shape)


def solution(mesh):
    ny = mesh.devices.shape[0]
    nz = 16
    nx = mesh.devices.shape[1] // nz // 2
    fine = Mesh(mesh.devices.reshape(ny, nx, nz, 2), ("y", "x", "z", "c"))
    ep = ("x", "z", "c")
    in_specs = (
        P(ep, None),
        P(ep, None),
        P(ep, None),
        P(ep, None, "y"),
        P(ep, None, "y"),
        P(ep, "y", None),
    )
    return jax.shard_map(
        per_device, mesh=fine, in_specs=in_specs, out_specs=P(ep, None), check_vma=False
    )
```

```python
import jax
import jax.numpy as jnp
from jax import lax
from jax.experimental import pallas as pl
from jax.experimental.pallas import tpu as pltpu
from jax.sharding import Mesh, PartitionSpec as P

BLOCK = 8
CAP = 2
SLOT = 8
MIB = 1 << 20


def params():
    return pltpu.CompilerParams(vmem_limit_bytes=24 * MIB)


def slot_mask(ids, experts):
    tokens, top = ids.shape
    lane = lax.broadcasted_iota(jnp.int32, (tokens, experts), 1)
    hit = jnp.zeros((tokens, experts), jnp.float32)
    for j in range(top):
        hit = hit + jnp.where(ids[:, j:j + 1] == lane, 1.0, 0.0)
    row = lax.broadcasted_iota(jnp.int32, (tokens, tokens), 0)
    col = lax.broadcasted_iota(jnp.int32, (tokens, tokens), 1)
    earlier = jnp.where((row // BLOCK == col // BLOCK) & (col < row), 1.0, 0.0).astype(jnp.bfloat16)
    rank = jnp.dot(earlier, hit.astype(jnp.bfloat16), preferred_element_type=jnp.float32)
    place = lax.broadcasted_iota(jnp.int32, (tokens, experts), 0) // BLOCK * CAP
    code = jnp.where(hit > 0.5, place.astype(jnp.float32) + rank + 1.0, 0.0)
    spread = expand(experts)
    wide = jnp.dot(code.astype(jnp.bfloat16), spread, preferred_element_type=jnp.float32)
    slot = lax.broadcasted_iota(jnp.int32, (tokens, experts * SLOT), 1) % SLOT
    return wide == (slot + 1).astype(jnp.float32)


def expand(experts):
    row = lax.broadcasted_iota(jnp.int32, (experts, experts * SLOT), 0)
    col = lax.broadcasted_iota(jnp.int32, (experts, experts * SLOT), 1)
    return jnp.where(col // SLOT == row, 1.0, 0.0).astype(jnp.bfloat16)


def dispatch_kernel(y_ref, ids_ref, tokens_ref, out_ref):
    experts = out_ref.shape[0] // SLOT
    count = tokens_ref.shape[0]
    row = lax.broadcasted_iota(jnp.int32, (count, count), 0)
    col = lax.broadcasted_iota(jnp.int32, (count, count), 1)
    unit = jnp.where(row == col, 1.0, 0.0).astype(jnp.bfloat16)
    across = ids_ref[...].astype(jnp.float32).astype(jnp.bfloat16)
    ids = lax.dot_general(
        unit, across, (((1,), (1,)), ((), ())), preferred_element_type=jnp.float32
    ).astype(jnp.int32)
    onehot = jnp.where(slot_mask(ids, experts), 1.0, 0.0).astype(jnp.bfloat16)
    rows = lax.dot_general(
        onehot, tokens_ref[...], (((0,), (0,)), ((), ())), preferred_element_type=jnp.float32
    )
    out_ref[...] = rows.astype(jnp.bfloat16)


def dispatch(y, ids, tokens, experts, width):
    count = tokens.shape[0]
    return pl.pallas_call(
        dispatch_kernel,
        grid_spec=pltpu.PrefetchScalarGridSpec(
            num_scalar_prefetch=1,
            grid=(1,),
            in_specs=[
                pl.BlockSpec(ids.shape, lambda i, y: (0, 0)),
                pl.BlockSpec((count, width), lambda i, y: (0, y[0])),
            ],
            out_specs=pl.BlockSpec((experts * SLOT, width), lambda i, y: (0, 0)),
        ),
        out_shape=jax.ShapeDtypeStruct((experts * SLOT, width), tokens.dtype),
        compiler_params=params(),
        name="dispatch_rows",
    )(y, ids, tokens)


def combine_kernel(y_ref, ids_ref, weight_ref, rows_ref, out_ref):
    experts = rows_ref.shape[0] // SLOT
    copies, count, features = out_ref.shape
    width = rows_ref.shape[1]
    quarters = features // width
    ids = jnp.concatenate([ids_ref[...]] * quarters, axis=0)
    weight = jnp.concatenate([weight_ref[...]] * quarters, axis=0)
    tokens, top = ids.shape
    mask = slot_mask(ids, experts)
    lane = lax.broadcasted_iota(jnp.int32, (tokens, experts), 1)
    rest = jnp.zeros((tokens, experts), jnp.float32)
    for j in range(top):
        rest = rest + jnp.where(ids[:, j:j + 1] == lane, weight[:, j:j + 1], 0.0)
    spread = expand(experts)
    total = None
    for _ in range(3):
        part = rest.astype(jnp.bfloat16)
        rest = rest - part.astype(jnp.float32)
        wide = jnp.dot(part, spread, preferred_element_type=jnp.float32)
        wide = jnp.where(mask, wide, 0.0).astype(jnp.bfloat16)
        term = jnp.dot(wide, rows_ref[...], preferred_element_type=jnp.float32)
        total = term if total is None else total + term
    line = jnp.concatenate([total[i * count:(i + 1) * count] for i in range(quarters)], axis=1)
    line = line.astype(jnp.bfloat16)
    for i in range(copies):
        out_ref[i] = line


def combine(y, ids, weight, rows, blocks):
    count, width = ids.shape[0] // blocks, rows.shape[1]
    shape = (blocks, count, blocks * width)
    return pl.pallas_call(
        combine_kernel,
        grid_spec=pltpu.PrefetchScalarGridSpec(
            num_scalar_prefetch=1,
            grid=(1,),
            in_specs=[
                pl.BlockSpec((count, ids.shape[1]), lambda i, y: (y[0], 0)),
                pl.BlockSpec((count, ids.shape[1]), lambda i, y: (y[0], 0)),
                pl.BlockSpec(rows.shape, lambda i, y: (0, 0)),
            ],
            out_specs=pl.BlockSpec(shape, lambda i, y: (0, 0, 0)),
        ),
        out_shape=jax.ShapeDtypeStruct(shape, jnp.bfloat16),
        compiler_params=params(),
        name="combine_rows",
    )(y, ids, weight, rows)


def regroup(rows, blocks, inverse):
    line = lax.broadcasted_iota(jnp.int32, (rows, 1), 0)
    span = rows // blocks
    if inverse:
        index = (line % SLOT) // CAP * span + line // SLOT * CAP + line % CAP
    else:
        index = (line % span) // CAP * SLOT + line // span * CAP + line % CAP
    hit = lax.broadcasted_iota(jnp.int32, (rows, rows), 1) == index
    return jnp.where(hit, 1.0, 0.0).astype(jnp.bfloat16)


def gate_up_kernel(q_ref, x_ref, w0_ref, w1_ref, out_ref, held):
    @pl.when(pl.program_id(0) == 0)
    def _():
        order = regroup(x_ref.shape[0], pl.num_programs(0), False)
        moved = jnp.dot(order, x_ref[...], preferred_element_type=jnp.float32)
        held[...] = moved.astype(jnp.bfloat16)

    hidden = w0_ref.shape[3]
    x = held[...]
    for c, ref in enumerate((w0_ref, w1_ref)):
        w = jnp.concatenate([ref[0, 0], ref[0, 1]], axis=1)
        part = jnp.dot(x, w, preferred_element_type=jnp.float32)
        out_ref[:, 2 * c * hidden:2 * (c + 1) * hidden] = part.astype(jnp.bfloat16)


def gate_up(q, rows, w_own, w_other):
    slots, width = rows.shape
    blocks, _, _, hidden = w_own.shape
    wide = pl.BlockSpec((1, 2, width, hidden), lambda i, q: (i, 0, 0, 0))
    return pl.pallas_call(
        gate_up_kernel,
        grid_spec=pltpu.PrefetchScalarGridSpec(
            num_scalar_prefetch=1,
            grid=(blocks,),
            in_specs=[pl.BlockSpec((slots, width), lambda i, q: (0, 0)), wide, wide],
            out_specs=pl.BlockSpec((slots, 4 * hidden), lambda i, q: (0, q[i])),
            scratch_shapes=[pltpu.VMEM((slots, width), jnp.bfloat16)],
        ),
        out_shape=jax.ShapeDtypeStruct((slots, 4 * blocks * hidden), jnp.bfloat16),
        compiler_params=params(),
        name="gate_up",
    )(q, rows, w_own, w_other)


def down_kernel(q_ref, x_ref, w0_ref, w1_ref, out_ref, act0, act1, held):
    step = pl.program_id(0)
    parts, span, columns = x_ref.shape
    group = columns // parts
    hidden = group // 4

    @pl.when(step == 0)
    def _():
        for i in range(parts):
            start = pl.multiple_of(q_ref[i] * group, group)
            total = None
            for p in range(parts):
                term = x_ref[p, :, pl.ds(start, group)].astype(jnp.float32)
                total = term if total is None else total + term
            for c, act in enumerate((act0, act1)):
                gate = total[:, 2 * c * hidden:(2 * c + 1) * hidden]
                up = total[:, (2 * c + 1) * hidden:(2 * c + 2) * hidden]
                value = gate / (1.0 + jnp.exp(-gate)) * up
                act[:, i * hidden:(i + 1) * hidden] = value.astype(jnp.bfloat16)

    total = jnp.dot(act0[...], w0_ref[...], preferred_element_type=jnp.float32)
    total = total + jnp.dot(act1[...], w1_ref[...], preferred_element_type=jnp.float32)
    held[pl.ds(pl.multiple_of(step * span, span), span)] = total.astype(jnp.bfloat16)

    @pl.when(step == parts - 1)
    def _():
        order = regroup(parts * span, parts, True)
        moved = jnp.dot(order, held[...], preferred_element_type=jnp.float32)
        out_ref[...] = moved.astype(jnp.bfloat16)


def down(q, sums, w_own, w_other):
    parts, span, _ = sums.shape
    depth, features = w_own.shape
    width = features // parts
    part = pl.BlockSpec((depth, width), lambda i, q: (0, i))
    return pl.pallas_call(
        down_kernel,
        grid_spec=pltpu.PrefetchScalarGridSpec(
            num_scalar_prefetch=1,
            grid=(parts,),
            in_specs=[pl.BlockSpec(sums.shape, lambda i, q: (0, 0, 0)), part, part],
            out_specs=pl.BlockSpec((parts * span, width), lambda i, q: (0, 0)),
            scratch_shapes=[
                pltpu.VMEM((span, depth), jnp.bfloat16),
                pltpu.VMEM((span, depth), jnp.bfloat16),
                pltpu.VMEM((parts * span, width), jnp.bfloat16),
            ],
        ),
        out_shape=jax.ShapeDtypeStruct((parts * span, width), jnp.bfloat16),
        compiler_params=params(),
        name="down_rows",
    )(q, sums, w_own, w_other)


def shift(block, step):
    n = lax.axis_size("y")
    return lax.ppermute(block, "y", [(i, (i + step) % n) for i in range(n)])


def swap(block):
    return lax.ppermute(block, "c", [(0, 1), (1, 0)])


def swap_all(block, axis):
    return lax.all_to_all(block, axis, split_axis=0, concat_axis=0, tiled=True)


def cut_kernel(q_ref, *refs):
    gates, ups, outs = refs[0:4], refs[4:8], refs[8:12]
    for gate, up, out in zip(gates, ups, outs):
        out[0] = gate[...]
        out[1] = up[...]


def cut(q, gate, up):
    depth, hidden = gate.shape
    width = depth // 4
    parts = [pl.BlockSpec((width, hidden), lambda s, q, i=i: (q[i], 0)) for i in range(4)]
    whole = pl.BlockSpec((2, width, hidden), lambda s, q: (0, 0, 0))
    return pl.pallas_call(
        cut_kernel,
        grid_spec=pltpu.PrefetchScalarGridSpec(
            num_scalar_prefetch=1, grid=(1,), in_specs=parts + parts, out_specs=[whole] * 4
        ),
        out_shape=[jax.ShapeDtypeStruct((2, width, hidden), gate.dtype)] * 4,
        compiler_params=params(),
        name="cut_quarters",
    )(q, *[gate] * 4, *[up] * 4)


def per_device(tokens, expert_ids, route_weight, w_gate, w_up, w_down):
    ny = lax.axis_size("y")
    experts = lax.axis_size("x") * lax.axis_size("z")
    y = lax.axis_index("y").astype(jnp.int32)
    q = jnp.stack([y, (y + 3) & 3, (y + 1) & 3, (y + 2) & 3])
    width = tokens.shape[1] // ny
    half = w_down.shape[1] // 2

    sent = dispatch(q[:1], expert_ids.T, tokens, experts, width)
    sent, w_gate, w_up, w_down = lax.optimization_barrier((sent, w_gate, w_up, w_down))
    rows = swap_all(sent, ("x", "z"))

    own, prior, later, across = cut(q, w_gate[0], w_up[0])
    pieces = [own, shift(later, 1), shift(prior, -1), shift(across, 2)]
    *pieces, w_down = lax.optimization_barrier((*pieces, w_down))
    both_own = jnp.stack(pieces)
    both_other = swap(both_own)

    before, after = shift(w_down[0], 1), shift(w_down[0], -1)
    relayed = (shift(before[:half], 1), shift(after[half:], -1))

    sums = gate_up(q, rows, both_own, both_other)
    sums, before, after, relayed = lax.optimization_barrier((sums, before, after, relayed))
    w_own = jnp.concatenate([w_down[0], before, after, *relayed], axis=0)
    w_other = swap(w_own)
    sums = swap_all(sums.reshape(ny, sums.shape[0] // ny, sums.shape[1]), "y")
    back = swap_all(down(q, sums, w_own, w_other), ("x", "z"))
    mine = swap_all(combine(q[:1], expert_ids, route_weight, back, ny), "y")
    return mine.reshape(tokens.shape)


def solution(mesh):
    ny = mesh.devices.shape[0]
    nz = 16
    nx = mesh.devices.shape[1] // nz // 2
    fine = Mesh(mesh.devices.reshape(ny, nx, nz, 2), ("y", "x", "z", "c"))
    ep = ("x", "z", "c")
    in_specs = (
        P(ep, None),
        P(ep, None),
        P(ep, None),
        P(ep, None, "y"),
        P(ep, None, "y"),
        P(ep, "y", None),
    )
    return jax.shard_map(
        per_device, mesh=fine, in_specs=in_specs, out_specs=P(ep, None), check_vma=False
    )
```

```python
import jax
import jax.numpy as jnp
from jax import lax
from jax.experimental import pallas as pl
from jax.experimental.pallas import tpu as pltpu
from jax.sharding import Mesh, PartitionSpec as P

BLOCK = 8
CAP = 2
SLOT = 8
MIB = 1 << 20


def params():
    return pltpu.CompilerParams(vmem_limit_bytes=24 * MIB)


def slot_mask(ids, experts):
    tokens, top = ids.shape
    lane = lax.broadcasted_iota(jnp.int32, (tokens, experts), 1)
    hit = jnp.zeros((tokens, experts), jnp.float32)
    for j in range(top):
        hit = hit + jnp.where(ids[:, j:j + 1] == lane, 1.0, 0.0)
    row = lax.broadcasted_iota(jnp.int32, (tokens, tokens), 0)
    col = lax.broadcasted_iota(jnp.int32, (tokens, tokens), 1)
    earlier = jnp.where((row // BLOCK == col // BLOCK) & (col < row), 1.0, 0.0).astype(jnp.bfloat16)
    rank = jnp.dot(earlier, hit.astype(jnp.bfloat16), preferred_element_type=jnp.float32)
    place = lax.broadcasted_iota(jnp.int32, (tokens, experts), 0) // BLOCK * CAP
    code = jnp.where(hit > 0.5, place.astype(jnp.float32) + rank + 1.0, 0.0)
    spread = expand(experts)
    wide = jnp.dot(code.astype(jnp.bfloat16), spread, preferred_element_type=jnp.float32)
    slot = lax.broadcasted_iota(jnp.int32, (tokens, experts * SLOT), 1) % SLOT
    return wide == (slot + 1).astype(jnp.float32)


def expand(experts):
    row = lax.broadcasted_iota(jnp.int32, (experts, experts * SLOT), 0)
    col = lax.broadcasted_iota(jnp.int32, (experts, experts * SLOT), 1)
    return jnp.where(col // SLOT == row, 1.0, 0.0).astype(jnp.bfloat16)


def dispatch_kernel(y_ref, ids_ref, tokens_ref, out_ref):
    experts = out_ref.shape[0] // SLOT
    count = tokens_ref.shape[0]
    row = lax.broadcasted_iota(jnp.int32, (count, count), 0)
    col = lax.broadcasted_iota(jnp.int32, (count, count), 1)
    unit = jnp.where(row == col, 1.0, 0.0).astype(jnp.bfloat16)
    across = ids_ref[...].astype(jnp.float32).astype(jnp.bfloat16)
    ids = lax.dot_general(
        unit, across, (((1,), (1,)), ((), ())), preferred_element_type=jnp.float32
    ).astype(jnp.int32)
    onehot = jnp.where(slot_mask(ids, experts), 1.0, 0.0).astype(jnp.bfloat16)
    rows = lax.dot_general(
        onehot, tokens_ref[...], (((0,), (0,)), ((), ())), preferred_element_type=jnp.float32
    )
    out_ref[...] = rows.astype(jnp.bfloat16)


def dispatch(y, ids, tokens, experts, width):
    count = tokens.shape[0]
    return pl.pallas_call(
        dispatch_kernel,
        grid_spec=pltpu.PrefetchScalarGridSpec(
            num_scalar_prefetch=1,
            grid=(1,),
            in_specs=[
                pl.BlockSpec(ids.shape, lambda i, y: (0, 0)),
                pl.BlockSpec((count, width), lambda i, y: (0, y[0])),
            ],
            out_specs=pl.BlockSpec((experts * SLOT, width), lambda i, y: (0, 0)),
        ),
        out_shape=jax.ShapeDtypeStruct((experts * SLOT, width), tokens.dtype),
        compiler_params=params(),
        name="dispatch_rows",
    )(y, ids, tokens)


def combine_kernel(y_ref, ids_ref, weight_ref, rows_ref, out_ref):
    experts = rows_ref.shape[0] // SLOT
    copies, count, features = out_ref.shape
    width = rows_ref.shape[1]
    quarters = features // width
    ids = jnp.concatenate([ids_ref[...]] * quarters, axis=0)
    weight = jnp.concatenate([weight_ref[...]] * quarters, axis=0)
    tokens, top = ids.shape
    mask = slot_mask(ids, experts)
    lane = lax.broadcasted_iota(jnp.int32, (tokens, experts), 1)
    rest = jnp.zeros((tokens, experts), jnp.float32)
    for j in range(top):
        rest = rest + jnp.where(ids[:, j:j + 1] == lane, weight[:, j:j + 1], 0.0)
    spread = expand(experts)
    total = None
    for _ in range(3):
        part = rest.astype(jnp.bfloat16)
        rest = rest - part.astype(jnp.float32)
        wide = jnp.dot(part, spread, preferred_element_type=jnp.float32)
        wide = jnp.where(mask, wide, 0.0).astype(jnp.bfloat16)
        term = jnp.dot(wide, rows_ref[...], preferred_element_type=jnp.float32)
        total = term if total is None else total + term
    line = jnp.concatenate([total[i * count:(i + 1) * count] for i in range(quarters)], axis=1)
    line = line.astype(jnp.bfloat16)
    for i in range(copies):
        out_ref[i] = line


def combine(y, ids, weight, rows, blocks):
    count, width = ids.shape[0] // blocks, rows.shape[1]
    shape = (blocks, count, blocks * width)
    return pl.pallas_call(
        combine_kernel,
        grid_spec=pltpu.PrefetchScalarGridSpec(
            num_scalar_prefetch=1,
            grid=(1,),
            in_specs=[
                pl.BlockSpec((count, ids.shape[1]), lambda i, y: (y[0], 0)),
                pl.BlockSpec((count, ids.shape[1]), lambda i, y: (y[0], 0)),
                pl.BlockSpec(rows.shape, lambda i, y: (0, 0)),
            ],
            out_specs=pl.BlockSpec(shape, lambda i, y: (0, 0, 0)),
        ),
        out_shape=jax.ShapeDtypeStruct(shape, jnp.bfloat16),
        compiler_params=params(),
        name="combine_rows",
    )(y, ids, weight, rows)


def regroup(rows, blocks, inverse):
    line = lax.broadcasted_iota(jnp.int32, (rows, 1), 0)
    span = rows // blocks
    if inverse:
        index = (line % SLOT) // CAP * span + line // SLOT * CAP + line % CAP
    else:
        index = (line % span) // CAP * SLOT + line // span * CAP + line % CAP
    hit = lax.broadcasted_iota(jnp.int32, (rows, rows), 1) == index
    return jnp.where(hit, 1.0, 0.0).astype(jnp.bfloat16)


def gate_up_kernel(q_ref, x_ref, w0_ref, w1_ref, out_ref, held):
    @pl.when(pl.program_id(0) == 0)
    def _():
        order = regroup(x_ref.shape[0], pl.num_programs(0), False)
        moved = jnp.dot(order, x_ref[...], preferred_element_type=jnp.float32)
        held[...] = moved.astype(jnp.bfloat16)

    hidden = w0_ref.shape[3]
    x = held[...]
    for c, ref in enumerate((w0_ref, w1_ref)):
        w = jnp.concatenate([ref[0, 0], ref[0, 1]], axis=1)
        part = jnp.dot(x, w, preferred_element_type=jnp.float32)
        out_ref[:, 2 * c * hidden:2 * (c + 1) * hidden] = part.astype(jnp.bfloat16)


def gate_up(q, rows, w_own, w_other):
    slots, width = rows.shape
    blocks, _, _, hidden = w_own.shape
    wide = pl.BlockSpec((1, 2, width, hidden), lambda i, q: (i, 0, 0, 0))
    return pl.pallas_call(
        gate_up_kernel,
        grid_spec=pltpu.PrefetchScalarGridSpec(
            num_scalar_prefetch=1,
            grid=(blocks,),
            in_specs=[pl.BlockSpec((slots, width), lambda i, q: (0, 0)), wide, wide],
            out_specs=pl.BlockSpec((slots, 4 * hidden), lambda i, q: (0, q[i])),
            scratch_shapes=[pltpu.VMEM((slots, width), jnp.bfloat16)],
        ),
        out_shape=jax.ShapeDtypeStruct((slots, 4 * blocks * hidden), jnp.bfloat16),
        compiler_params=params(),
        name="gate_up",
    )(q, rows, w_own, w_other)


def down_kernel(q_ref, x_ref, w0_ref, w1_ref, out_ref, act0, act1, held):
    step = pl.program_id(0)
    parts, span, columns = x_ref.shape
    group = columns // parts
    hidden = group // 4

    @pl.when(step == 0)
    def _():
        for i in range(parts):
            start = pl.multiple_of(q_ref[i] * group, group)
            total = None
            for p in range(parts):
                term = x_ref[p, :, pl.ds(start, group)].astype(jnp.float32)
                total = term if total is None else total + term
            for c, act in enumerate((act0, act1)):
                gate = total[:, 2 * c * hidden:(2 * c + 1) * hidden]
                up = total[:, (2 * c + 1) * hidden:(2 * c + 2) * hidden]
                value = gate / (1.0 + jnp.exp(-gate)) * up
                act[:, i * hidden:(i + 1) * hidden] = value.astype(jnp.bfloat16)

    total = jnp.dot(act0[...], w0_ref[...], preferred_element_type=jnp.float32)
    total = total + jnp.dot(act1[...], w1_ref[...], preferred_element_type=jnp.float32)
    held[pl.ds(pl.multiple_of(step * span, span), span)] = total.astype(jnp.bfloat16)

    @pl.when(step == parts - 1)
    def _():
        order = regroup(parts * span, parts, True)
        moved = jnp.dot(order, held[...], preferred_element_type=jnp.float32)
        out_ref[...] = moved.astype(jnp.bfloat16)


def down(q, sums, w_own, w_other):
    parts, span, _ = sums.shape
    depth, features = w_own.shape
    width = features // parts
    part = pl.BlockSpec((depth, width), lambda i, q: (0, i))
    return pl.pallas_call(
        down_kernel,
        grid_spec=pltpu.PrefetchScalarGridSpec(
            num_scalar_prefetch=1,
            grid=(parts,),
            in_specs=[pl.BlockSpec(sums.shape, lambda i, q: (0, 0, 0)), part, part],
            out_specs=pl.BlockSpec((parts * span, width), lambda i, q: (0, 0)),
            scratch_shapes=[
                pltpu.VMEM((span, depth), jnp.bfloat16),
                pltpu.VMEM((span, depth), jnp.bfloat16),
                pltpu.VMEM((parts * span, width), jnp.bfloat16),
            ],
        ),
        out_shape=jax.ShapeDtypeStruct((parts * span, width), jnp.bfloat16),
        compiler_params=params(),
        name="down_rows",
    )(q, sums, w_own, w_other)


def shift(block, step):
    n = lax.axis_size("y")
    return lax.ppermute(block, "y", [(i, (i + step) % n) for i in range(n)])


def swap(block):
    return lax.ppermute(block, "c", [(0, 1), (1, 0)])


def swap_all(block, axis):
    return lax.all_to_all(block, axis, split_axis=0, concat_axis=0, tiled=True)


def cut_kernel(q_ref, *refs):
    gates, ups, outs = refs[0:4], refs[4:8], refs[8:12]
    for gate, up, out in zip(gates, ups, outs):
        out[0] = gate[...]
        out[1] = up[...]


def cut(q, gate, up):
    depth, hidden = gate.shape
    width = depth // 4
    parts = [pl.BlockSpec((width, hidden), lambda s, q, i=i: (q[i], 0)) for i in range(4)]
    whole = pl.BlockSpec((2, width, hidden), lambda s, q: (0, 0, 0))
    return pl.pallas_call(
        cut_kernel,
        grid_spec=pltpu.PrefetchScalarGridSpec(
            num_scalar_prefetch=1, grid=(1,), in_specs=parts + parts, out_specs=[whole] * 4
        ),
        out_shape=[jax.ShapeDtypeStruct((2, width, hidden), gate.dtype)] * 4,
        compiler_params=params(),
        name="cut_quarters",
    )(q, *[gate] * 4, *[up] * 4)


def per_device(tokens, expert_ids, route_weight, w_gate, w_up, w_down):
    ny = lax.axis_size("y")
    experts = lax.axis_size("x") * lax.axis_size("z")
    y = lax.axis_index("y").astype(jnp.int32)
    q = jnp.stack([y, (y + 3) & 3, (y + 1) & 3, (y + 2) & 3])
    width = tokens.shape[1] // ny
    half = w_down.shape[1] // 2

    sent = dispatch(q[:1], expert_ids.T, tokens, experts, width)
    sent, w_gate, w_up, w_down = lax.optimization_barrier((sent, w_gate, w_up, w_down))
    rows = swap_all(sent, ("x", "z"))

    cuts = cut(q, w_gate[0], w_up[0])
    own, prior, later, across, w_down = lax.optimization_barrier((*cuts, w_down))
    pieces = [own, shift(later, 1), shift(prior, -1), shift(across, 2)]
    both_own = jnp.stack(pieces)
    both_other = swap(both_own)

    before, after = shift(w_down[0], 1), shift(w_down[0], -1)
    relayed = (shift(before[:half], 1), shift(after[half:], -1))

    sums = gate_up(q, rows, both_own, both_other)
    sums, before, after, relayed = lax.optimization_barrier((sums, before, after, relayed))
    w_own = jnp.concatenate([w_down[0], before, after, *relayed], axis=0)
    w_other = swap(w_own)
    sums = swap_all(sums.reshape(ny, sums.shape[0] // ny, sums.shape[1]), "y")
    back = swap_all(down(q, sums, w_own, w_other), ("x", "z"))
    mine = swap_all(combine(q[:1], expert_ids, route_weight, back, ny), "y")
    return mine.reshape(tokens.shape)


def solution(mesh):
    ny = mesh.devices.shape[0]
    nz = 16
    nx = mesh.devices.shape[1] // nz // 2
    fine = Mesh(mesh.devices.reshape(ny, nx, nz, 2), ("y", "x", "z", "c"))
    ep = ("x", "z", "c")
    in_specs = (
        P(ep, None),
        P(ep, None),
        P(ep, None),
        P(ep, None, "y"),
        P(ep, None, "y"),
        P(ep, "y", None),
    )
    return jax.shard_map(
        per_device, mesh=fine, in_specs=in_specs, out_specs=P(ep, None), check_vma=False
    )
```

```python
import jax
import jax.numpy as jnp
from jax import lax
from jax.experimental import pallas as pl
from jax.experimental.pallas import tpu as pltpu
from jax.sharding import Mesh, PartitionSpec as P

BLOCK = 8
CAP = 2
SLOT = 8
MIB = 1 << 20


def params(limit=24):
    return pltpu.CompilerParams(vmem_limit_bytes=limit * MIB)


def slot_mask(ids, experts):
    tokens, top = ids.shape
    lane = lax.broadcasted_iota(jnp.int32, (tokens, experts), 1)
    hit = jnp.zeros((tokens, experts), jnp.float32)
    for j in range(top):
        hit = hit + jnp.where(ids[:, j:j + 1] == lane, 1.0, 0.0)
    row = lax.broadcasted_iota(jnp.int32, (tokens, tokens), 0)
    col = lax.broadcasted_iota(jnp.int32, (tokens, tokens), 1)
    earlier = jnp.where((row // BLOCK == col // BLOCK) & (col < row), 1.0, 0.0).astype(jnp.bfloat16)
    rank = jnp.dot(earlier, hit.astype(jnp.bfloat16), preferred_element_type=jnp.float32)
    place = lax.broadcasted_iota(jnp.int32, (tokens, experts), 0) // BLOCK * CAP
    code = jnp.where(hit > 0.5, place.astype(jnp.float32) + rank + 1.0, 0.0)
    spread = expand(experts)
    wide = jnp.dot(code.astype(jnp.bfloat16), spread, preferred_element_type=jnp.float32)
    slot = lax.broadcasted_iota(jnp.int32, (tokens, experts * SLOT), 1) % SLOT
    return wide == (slot + 1).astype(jnp.float32)


def expand(experts):
    row = lax.broadcasted_iota(jnp.int32, (experts, experts * SLOT), 0)
    col = lax.broadcasted_iota(jnp.int32, (experts, experts * SLOT), 1)
    return jnp.where(col // SLOT == row, 1.0, 0.0).astype(jnp.bfloat16)


def dispatch_kernel(y_ref, ids_ref, tokens_ref, out_ref):
    experts = out_ref.shape[0] // SLOT
    count = tokens_ref.shape[0]
    row = lax.broadcasted_iota(jnp.int32, (count, count), 0)
    col = lax.broadcasted_iota(jnp.int32, (count, count), 1)
    unit = jnp.where(row == col, 1.0, 0.0).astype(jnp.bfloat16)
    across = ids_ref[...].astype(jnp.float32).astype(jnp.bfloat16)
    ids = lax.dot_general(
        unit, across, (((1,), (1,)), ((), ())), preferred_element_type=jnp.float32
    ).astype(jnp.int32)
    onehot = jnp.where(slot_mask(ids, experts), 1.0, 0.0).astype(jnp.bfloat16)
    rows = lax.dot_general(
        onehot, tokens_ref[...], (((0,), (0,)), ((), ())), preferred_element_type=jnp.float32
    )
    out_ref[...] = rows.astype(jnp.bfloat16)


def dispatch(y, ids, tokens, experts, width):
    count = tokens.shape[0]
    return pl.pallas_call(
        dispatch_kernel,
        grid_spec=pltpu.PrefetchScalarGridSpec(
            num_scalar_prefetch=1,
            grid=(1,),
            in_specs=[
                pl.BlockSpec(ids.shape, lambda i, y: (0, 0)),
                pl.BlockSpec((count, width), lambda i, y: (0, y[0])),
            ],
            out_specs=pl.BlockSpec((experts * SLOT, width), lambda i, y: (0, 0)),
        ),
        out_shape=jax.ShapeDtypeStruct((experts * SLOT, width), tokens.dtype),
        compiler_params=params(60),
        name="dispatch_rows",
    )(y, ids, tokens)


def combine_kernel(y_ref, ids_ref, weight_ref, rows_ref, out_ref):
    experts = rows_ref.shape[0] // SLOT
    copies, count, features = out_ref.shape
    width = rows_ref.shape[1]
    quarters = features // width
    ids = jnp.concatenate([ids_ref[...]] * quarters, axis=0)
    weight = jnp.concatenate([weight_ref[...]] * quarters, axis=0)
    tokens, top = ids.shape
    mask = slot_mask(ids, experts)
    lane = lax.broadcasted_iota(jnp.int32, (tokens, experts), 1)
    rest = jnp.zeros((tokens, experts), jnp.float32)
    for j in range(top):
        rest = rest + jnp.where(ids[:, j:j + 1] == lane, weight[:, j:j + 1], 0.0)
    spread = expand(experts)
    total = None
    for _ in range(3):
        part = rest.astype(jnp.bfloat16)
        rest = rest - part.astype(jnp.float32)
        wide = jnp.dot(part, spread, preferred_element_type=jnp.float32)
        wide = jnp.where(mask, wide, 0.0).astype(jnp.bfloat16)
        term = jnp.dot(wide, rows_ref[...], preferred_element_type=jnp.float32)
        total = term if total is None else total + term
    line = jnp.concatenate([total[i * count:(i + 1) * count] for i in range(quarters)], axis=1)
    line = line.astype(jnp.bfloat16)
    for i in range(copies):
        out_ref[i] = line


def combine(y, ids, weight, rows, blocks):
    count, width = ids.shape[0] // blocks, rows.shape[1]
    shape = (blocks, count, blocks * width)
    return pl.pallas_call(
        combine_kernel,
        grid_spec=pltpu.PrefetchScalarGridSpec(
            num_scalar_prefetch=1,
            grid=(1,),
            in_specs=[
                pl.BlockSpec((count, ids.shape[1]), lambda i, y: (y[0], 0)),
                pl.BlockSpec((count, ids.shape[1]), lambda i, y: (y[0], 0)),
                pl.BlockSpec(rows.shape, lambda i, y: (0, 0)),
            ],
            out_specs=pl.BlockSpec(shape, lambda i, y: (0, 0, 0)),
        ),
        out_shape=jax.ShapeDtypeStruct(shape, jnp.bfloat16),
        compiler_params=params(),
        name="combine_rows",
    )(y, ids, weight, rows)


def regroup(rows, blocks, inverse):
    line = lax.broadcasted_iota(jnp.int32, (rows, 1), 0)
    span = rows // blocks
    if inverse:
        index = (line % SLOT) // CAP * span + line // SLOT * CAP + line % CAP
    else:
        index = (line % span) // CAP * SLOT + line // span * CAP + line % CAP
    hit = lax.broadcasted_iota(jnp.int32, (rows, rows), 1) == index
    return jnp.where(hit, 1.0, 0.0).astype(jnp.bfloat16)


def gate_up_kernel(q_ref, x_ref, w0_ref, w1_ref, out_ref, held):
    @pl.when(pl.program_id(0) == 0)
    def _():
        order = regroup(x_ref.shape[0], pl.num_programs(0), False)
        moved = jnp.dot(order, x_ref[...], preferred_element_type=jnp.float32)
        held[...] = moved.astype(jnp.bfloat16)

    hidden = w0_ref.shape[3]
    x = held[...]
    for c, ref in enumerate((w0_ref, w1_ref)):
        w = jnp.concatenate([ref[0, 0], ref[0, 1]], axis=1)
        part = jnp.dot(x, w, preferred_element_type=jnp.float32)
        out_ref[:, 2 * c * hidden:2 * (c + 1) * hidden] = part.astype(jnp.bfloat16)


def gate_up(q, rows, w_own, w_other):
    slots, width = rows.shape
    blocks, _, _, hidden = w_own.shape
    wide = pl.BlockSpec((1, 2, width, hidden), lambda i, q: (i, 0, 0, 0))
    return pl.pallas_call(
        gate_up_kernel,
        grid_spec=pltpu.PrefetchScalarGridSpec(
            num_scalar_prefetch=1,
            grid=(blocks,),
            in_specs=[pl.BlockSpec((slots, width), lambda i, q: (0, 0)), wide, wide],
            out_specs=pl.BlockSpec((slots, 4 * hidden), lambda i, q: (0, q[i])),
            scratch_shapes=[pltpu.VMEM((slots, width), jnp.bfloat16)],
        ),
        out_shape=jax.ShapeDtypeStruct((slots, 4 * blocks * hidden), jnp.bfloat16),
        compiler_params=params(),
        name="gate_up",
    )(q, rows, w_own, w_other)


def down_kernel(q_ref, x_ref, w0_ref, w1_ref, out_ref, act0, act1, held):
    step = pl.program_id(0)
    parts, span, columns = x_ref.shape
    group = columns // parts
    hidden = group // 4

    @pl.when(step == 0)
    def _():
        for i in range(parts):
            start = pl.multiple_of(q_ref[i] * group, group)
            total = None
            for p in range(parts):
                term = x_ref[p, :, pl.ds(start, group)].astype(jnp.float32)
                total = term if total is None else total + term
            for c, act in enumerate((act0, act1)):
                gate = total[:, 2 * c * hidden:(2 * c + 1) * hidden]
                up = total[:, (2 * c + 1) * hidden:(2 * c + 2) * hidden]
                value = gate / (1.0 + jnp.exp(-gate)) * up
                act[:, i * hidden:(i + 1) * hidden] = value.astype(jnp.bfloat16)

    total = jnp.dot(act0[...], w0_ref[...], preferred_element_type=jnp.float32)
    total = total + jnp.dot(act1[...], w1_ref[...], preferred_element_type=jnp.float32)
    held[pl.ds(pl.multiple_of(step * span, span), span)] = total.astype(jnp.bfloat16)

    @pl.when(step == parts - 1)
    def _():
        order = regroup(parts * span, parts, True)
        moved = jnp.dot(order, held[...], preferred_element_type=jnp.float32)
        out_ref[...] = moved.astype(jnp.bfloat16)


def down(q, sums, w_own, w_other):
    parts, span, _ = sums.shape
    depth, features = w_own.shape
    width = features // parts
    part = pl.BlockSpec((depth, width), lambda i, q: (0, i))
    return pl.pallas_call(
        down_kernel,
        grid_spec=pltpu.PrefetchScalarGridSpec(
            num_scalar_prefetch=1,
            grid=(parts,),
            in_specs=[pl.BlockSpec(sums.shape, lambda i, q: (0, 0, 0)), part, part],
            out_specs=pl.BlockSpec((parts * span, width), lambda i, q: (0, 0)),
            scratch_shapes=[
                pltpu.VMEM((span, depth), jnp.bfloat16),
                pltpu.VMEM((span, depth), jnp.bfloat16),
                pltpu.VMEM((parts * span, width), jnp.bfloat16),
            ],
        ),
        out_shape=jax.ShapeDtypeStruct((parts * span, width), jnp.bfloat16),
        compiler_params=params(),
        name="down_rows",
    )(q, sums, w_own, w_other)


def shift(block, step):
    n = lax.axis_size("y")
    return lax.ppermute(block, "y", [(i, (i + step) % n) for i in range(n)])


def swap(block):
    return lax.ppermute(block, "c", [(0, 1), (1, 0)])


def swap_all(block, axis):
    return lax.all_to_all(block, axis, split_axis=0, concat_axis=0, tiled=True)


def cut_kernel(q_ref, *refs):
    gates, ups, outs = refs[0:4], refs[4:8], refs[8:12]
    for gate, up, out in zip(gates, ups, outs):
        out[0] = gate[...]
        out[1] = up[...]


def cut(q, gate, up):
    depth, hidden = gate.shape
    width = depth // 4
    parts = [pl.BlockSpec((width, hidden), lambda s, q, i=i: (q[i], 0)) for i in range(4)]
    whole = pl.BlockSpec((2, width, hidden), lambda s, q: (0, 0, 0))
    return pl.pallas_call(
        cut_kernel,
        grid_spec=pltpu.PrefetchScalarGridSpec(
            num_scalar_prefetch=1, grid=(1,), in_specs=parts + parts, out_specs=[whole] * 4
        ),
        out_shape=[jax.ShapeDtypeStruct((2, width, hidden), gate.dtype)] * 4,
        compiler_params=params(60),
        name="cut_quarters",
    )(q, *[gate] * 4, *[up] * 4)


def per_device(tokens, expert_ids, route_weight, w_gate, w_up, w_down):
    ny = lax.axis_size("y")
    experts = lax.axis_size("x") * lax.axis_size("z")
    y = lax.axis_index("y").astype(jnp.int32)
    q = jnp.stack([y, (y + 3) & 3, (y + 1) & 3, (y + 2) & 3])
    width = tokens.shape[1] // ny
    half = w_down.shape[1] // 2

    sent = dispatch(q[:1], expert_ids.T, tokens, experts, width)
    sent, w_gate, w_up, w_down = lax.optimization_barrier((sent, w_gate, w_up, w_down))
    rows = swap_all(sent, ("x", "z"))

    cuts = cut(q, w_gate[0], w_up[0])
    own, prior, later, across, w_down = lax.optimization_barrier((*cuts, w_down))
    pieces = [own, shift(later, 1), shift(prior, -1), shift(across, 2)]
    both_own = jnp.stack(pieces)
    both_other = swap(both_own)

    before, after = shift(w_down[0], 1), shift(w_down[0], -1)
    relayed = (shift(before[:half], 1), shift(after[half:], -1))

    sums = gate_up(q, rows, both_own, both_other)
    sums, before, after, relayed = lax.optimization_barrier((sums, before, after, relayed))
    w_own = jnp.concatenate([w_down[0], before, after, *relayed], axis=0)
    w_other = swap(w_own)
    sums = swap_all(sums.reshape(ny, sums.shape[0] // ny, sums.shape[1]), "y")
    back = swap_all(down(q, sums, w_own, w_other), ("x", "z"))
    mine = swap_all(combine(q[:1], expert_ids, route_weight, back, ny), "y")
    return mine.reshape(tokens.shape)


def solution(mesh):
    ny = mesh.devices.shape[0]
    nz = 16
    nx = mesh.devices.shape[1] // nz // 2
    fine = Mesh(mesh.devices.reshape(ny, nx, nz, 2), ("y", "x", "z", "c"))
    ep = ("x", "z", "c")
    in_specs = (
        P(ep, None),
        P(ep, None),
        P(ep, None),
        P(ep, None, "y"),
        P(ep, None, "y"),
        P(ep, "y", None),
    )
    return jax.shard_map(
        per_device, mesh=fine, in_specs=in_specs, out_specs=P(ep, None), check_vma=False
    )
```
